128 devices in a mesh: seq: 32 (over x, y, core), col: 4 (over z).
Axes of the slice: x: 4, y: 4, z: 4, core: 2. Of those that a mesh axis runs over, the one named last changes fastest.
Arguments:
- atoms: bfloat16 [16384, 128], P(('seq', 'col')), may hold values from -6 to 6
- cotangent: bfloat16 [16384, 128], P(('seq', 'col')), may hold values from -6 to 6
- token_counts: int32 [128, 16], replicated, may hold values from 1 to 24, 128 in all within a row
- pair: bfloat16 [2048, 2048, 128], P('seq', 'col'), may hold values from -450 to 450
- w_qkvg: bfloat16 [3, 128, 512], replicated, may hold values from -0.5 to 0.5
- w_out: bfloat16 [3, 128, 128], replicated, may hold values from -0.5 to 0.5
- w_up: bfloat16 [3, 128, 512], replicated, may hold values from -0.5 to 0.5
- w_down: bfloat16 [3, 256, 128], replicated, may hold values from -0.375 to 0.375
- w_pair: bfloat16 [128, 12], replicated, may hold values from -2 to 2
Outputs:
- out_atoms: bfloat16 [16384, 128], P(('seq', 'col'))
- grad_atoms: bfloat16 [16384, 128], P(('seq', 'col'))
- grad_pair: bfloat16 [2048, 2048, 128], P('seq', 'col')
- grad_qkvg: float32 [3, 128, 512], replicated
- grad_out: float32 [3, 128, 128], replicated
- grad_up: float32 [3, 128, 512], replicated
- grad_down: float32 [3, 256, 128], replicated
- grad_pair_w: float32 [128, 12], replicated
The draws below stay inside these ranges and needn't reach their ends.
Inputs may be any that keep to these rules, and one draw needn't show every extreme that they name: `token_counts`: each row sums to 128.
All inputs are finite; a program needn't handle non-finite values.
Results may differ from the reference program's by a relative error of at most 0.03.
Values may be sent and summed in bfloat16 or wider, within the bound.
A program may use at most 128 MiB of HBM per device.

```python
import math
import jax
import jax.numpy as jnp
import numpy as np
from jax import lax

D = 128
HEADS = 4
CPAIR = 128
FF = 256
LAYERS = 3
Q_BLOCK = 32
K_BLOCK = 128
HALO = 48
BLK_DEV = 4
ATOM_DEV = 128
TOK_DEV = 16
MOST = 24
ATOMS = 16384
NTOK = 2048
N_SEQ = 32
N_COL = 4


def draw_pair(key, part):
    key = jax.random.fold_in(key, 7)
    normal_key = jax.random.fold_in(key, 0)
    values = jax.random.truncated_normal(normal_key, -6.0, 6.0, (NTOK, NTOK, CPAIR), jnp.float32) * 0.25
    return values.astype(jnp.bfloat16)


def steps_of(stream_key, dims, cuts, low, top_value):
    def one(dim, parts):
        draws = jax.random.uniform(jax.random.fold_in(jax.random.fold_in(stream_key, 6), dim), (parts,), jnp.float32, low / len(cuts), top_value / len(cuts))
        return jnp.repeat(jnp.exp(draws), dims[dim] // parts).reshape((-1,) + (1,) * (len(dims) - dim - 1))

    loudness = one(*cuts[0])
    for cut in cuts[1:]:
        loudness = loudness * one(*cut)
    return loudness


def split_up(amount, total, reach, skew):
    loads = [(1 << 20) // math.isqrt(rank ** skew) + 1 for rank in range(2, amount + 1)]
    surplus, counts = total - reach - (amount - 1), [1] * (amount - 1)
    while surplus > 0:
        candidates = [i for i in range(amount - 1) if counts[i] < reach]
        whole, budget = sum([loads[i] for i in candidates]), surplus
        for i in candidates:
            extra = min(reach - counts[i], max(1, budget * loads[i] // whole), surplus)
            counts[i] = counts[i] + extra
            surplus = surplus - extra
    return np.array([reach] + counts)


def uneven_parts(own_key, amount, total, bound, skew):
    if amount == 2:
        one = jax.random.randint(own_key, (), max(1, total - bound), min(bound, total - 1) + 1)
        return jnp.stack([one, total - one])
    sizes = jnp.asarray(split_up(amount, total, bound, skew), jnp.int32)
    couples = (amount - 1) // 2
    giver, sink = sizes[1:1 + 2 * couples:2], sizes[2:2 + 2 * couples:2]
    slack = jnp.minimum(giver - 1, bound - sink)
    moved = jax.random.randint(jax.random.fold_in(own_key, 1), (couples,), 0, 1 << 20) % (slack + 1)
    sizes = sizes.at[1:1 + 2 * couples:2].set(giver - moved).at[2:2 + 2 * couples:2].set(sink + moved)
    return sizes[jax.random.permutation(jax.random.fold_in(own_key, 2), amount)]


def scatter_about(rng, extent, scale, bound, pieces=(), held_as=jnp.bfloat16):
    level = steps_of(rng, extent, pieces, -0.22, 0.18) if pieces else 1.0
    values = jax.random.normal(rng, extent, jnp.float32) * scale * level
    return jnp.minimum(jnp.maximum(values, -bound), bound).astype(held_as)


def setup_inputs(seed: int = 0) -> dict:
    key_list = jax.random.split(jax.random.key(seed), 10)
    return {
        "atoms": scatter_about(key_list[0], (ATOMS, D), 1.0, 6.0, ((0, 128),)),
        "cotangent": scatter_about(key_list[1], (ATOMS, D), 1.0, 6.0, ((0, 128),)),
        "token_counts": jax.vmap(lambda own: uneven_parts(own, TOK_DEV, ATOM_DEV, MOST, 2))(jax.random.split(key_list[2], (N_SEQ * N_COL))).reshape((N_SEQ * N_COL, TOK_DEV)).astype(jnp.int32),
        "pair": draw_pair(jax.random.fold_in(key_list[9], 71), 0),
        "w_qkvg": scatter_about(key_list[4], (LAYERS, D, 4 * D), D ** -0.5, 0.5),
        "w_out": scatter_about(key_list[5], (LAYERS, D, D), D ** -0.5, 0.5),
        "w_up": scatter_about(key_list[6], (LAYERS, D, 2 * FF), D ** -0.5, 0.5),
        "w_down": scatter_about(key_list[7], (LAYERS, FF, D), FF ** -0.5, 0.375),
        "w_pair": scatter_about(key_list[8], (CPAIR, LAYERS * HEADS), (CPAIR // 16) ** -0.5, 2.0),
    }


def layer_norm(vector):
    average = lax.optimization_barrier(jnp.mean(vector, axis=-1, keepdims=True))
    centred = vector - average
    spread = lax.optimization_barrier(jnp.mean(centred * centred, axis=-1, keepdims=True))
    return centred * lax.rsqrt(spread + 1e-05)

def project(resid_in, offset, w_qkvg_l):
    normed = layer_norm(resid_in).astype(jnp.bfloat16)
    pre_act = jnp.dot(normed, w_qkvg_l, preferred_element_type=jnp.float32) + offset
    feature_width = resid_in.shape[1]
    queries = pre_act[:, :feature_width].astype(jnp.bfloat16)
    key_value = pre_act[:, feature_width:3 * feature_width].astype(jnp.bfloat16)
    queries, key_value = lax.optimization_barrier((queries, key_value))
    gate_act = jax.nn.sigmoid(pre_act[:, 3 * feature_width:])
    return ((queries, key_value, gate_act), normed)

def attend(queries, windows, bias, key_valid):
    blocks = windows.shape[0]
    head_count = bias.shape[1]
    feature_width = queries.shape[1]
    head_dim = feature_width // head_count
    query_part = queries.astype(jnp.bfloat16).astype(jnp.float32).reshape(blocks, Q_BLOCK, head_count, head_dim)
    window_half = windows.astype(jnp.bfloat16).astype(jnp.float32)
    key_part = window_half[:, :, :feature_width].reshape(blocks, K_BLOCK, head_count, head_dim)
    value_part = window_half[:, :, feature_width:].reshape(blocks, K_BLOCK, head_count, head_dim)
    scores = jnp.einsum('bihd,bkhd->bhik', query_part, key_part, preferred_element_type=jnp.float32)
    scores = scores * (1.0 / math.sqrt(head_dim)) + bias
    scores = jnp.where(key_valid[:, None, None, :], scores, -1e+30)
    largest = lax.stop_gradient(lax.optimization_barrier(jnp.max(scores, axis=-1, keepdims=True)))
    weights = jnp.exp(scores - largest)
    weights = (weights / lax.optimization_barrier(jnp.sum(weights, axis=-1, keepdims=True))).astype(jnp.bfloat16)
    mixed = jnp.einsum('bhik,bkhd->bihd', weights.astype(jnp.float32), value_part, preferred_element_type=jnp.float32)
    return mixed.reshape(blocks * Q_BLOCK, feature_width)

def finish(mixed, gate_act, resid_in, offsets, w_out_l, w_up_l, w_down_l):
    hidden_width = w_down_l.shape[0]
    gated = (mixed * gate_act).astype(jnp.bfloat16)
    attn_sum = jnp.dot(gated, w_out_l, preferred_element_type=jnp.float32) + offsets[1]
    residual = resid_in + attn_sum
    normed_two = layer_norm(residual).astype(jnp.bfloat16)
    up_both = jnp.dot(normed_two, w_up_l, preferred_element_type=jnp.float32) + offsets[2]
    hidden = (jax.nn.silu(up_both[:, :hidden_width]) * up_both[:, hidden_width:]).astype(jnp.bfloat16)
    result = residual + jnp.dot(hidden, w_down_l, preferred_element_type=jnp.float32) + offsets[3]
    return (result.astype(jnp.bfloat16), (gated, normed_two, hidden))

def layer_global(current, bias, key_valid, offsets, w_qkvg_l, w_out_l, w_up_l, w_down_l):
    resid_in = current.astype(jnp.float32)
    (queries, key_value, gate_act), normed = project(resid_in, offsets[0], w_qkvg_l)
    padded = jnp.pad(key_value.astype(jnp.float32), ((HALO, HALO), (0, 0)))
    blocks = bias.shape[0]
    window_index = jnp.arange(blocks, dtype=jnp.int32)[:, None] * Q_BLOCK + jnp.arange(K_BLOCK, dtype=jnp.int32)[None, :]
    windows = padded[window_index]
    mixed = attend(queries.astype(jnp.float32), windows, bias, key_valid)
    result, (gated, normed_two, hidden) = finish(mixed, gate_act, resid_in, offsets, w_out_l, w_up_l, w_down_l)
    return (result, (normed, gated, normed_two, hidden))

def pick_table(table, query_rows, key_cols):
    return table[:, query_rows[:, None], key_cols[None, :]]

def outer_sum(left, right):
    return jnp.dot(left.astype(jnp.float32).T, right, precision=lax.Precision.HIGHEST)

def reference(atoms, cotangent, token_counts, pair, w_qkvg, w_out, w_up, w_down, w_pair):
    groups = N_SEQ * N_COL
    blocks = ATOMS // Q_BLOCK
    token_ends = jnp.cumsum(token_counts, axis=1).astype(jnp.int32)
    position = jnp.arange(ATOM_DEV, dtype=jnp.int32)
    local_token = lax.optimization_barrier(jnp.sum((token_ends[:, None, :] <= position[None, :, None]).astype(jnp.int32), axis=2)).astype(jnp.int32)
    global_token = (local_token + TOK_DEV * jnp.arange(groups, dtype=jnp.int32)[:, None]).reshape(ATOMS)
    block_group = jnp.arange(blocks, dtype=jnp.int32) // BLK_DEV
    query_token = global_token.reshape(blocks, Q_BLOCK) - TOK_DEV * block_group[:, None]
    key_position = jnp.arange(blocks, dtype=jnp.int32)[:, None] * Q_BLOCK - HALO + jnp.arange(K_BLOCK, dtype=jnp.int32)[None, :]
    key_valid = (key_position >= 0) & (key_position < ATOMS)
    key_token = global_token[jnp.clip(key_position, 0, ATOMS - 1)] - TOK_DEV * (block_group[:, None] - 1)
    key_token = jnp.where(key_valid, key_token, 0).astype(jnp.int32)

    def pair_tile(group_index):
        row_block = lax.dynamic_slice_in_dim(pair, (group_index * TOK_DEV).astype(jnp.int32), TOK_DEV, 0)
        columns = group_index * TOK_DEV - TOK_DEV + jnp.arange(3 * TOK_DEV, dtype=jnp.int32)
        inside = (columns >= 0) & (columns < NTOK)
        taken = jnp.take(row_block, jnp.clip(columns, 0, NTOK - 1).astype(jnp.int32), axis=1)
        return jnp.where(inside[None, :, None], taken, jnp.zeros_like(taken))
    tiles_half = lax.map(pair_tile, jnp.arange(groups, dtype=jnp.int32))
    tiles = tiles_half.astype(jnp.float32)
    w_pair32 = w_pair.astype(jnp.float32)
    projected = jnp.einsum('gtuc,ch->ghtu', tiles, w_pair32, preferred_element_type=jnp.float32)
    zero_sets = []
    for layer_index in range(LAYERS):
        zero_sets.append((jnp.zeros((ATOMS, 4 * D), jnp.float32), jnp.zeros((ATOMS, D), jnp.float32), jnp.zeros((ATOMS, 2 * FF), jnp.float32), jnp.zeros((ATOMS, D), jnp.float32)))

    def forward(atoms_in, projected_in, offsets_all):
        per_block = projected_in[block_group]
        bias_all = jax.vmap(pick_table)(per_block, query_token, key_token)
        current = atoms_in
        saved = []
        for layer_index in range(LAYERS):
            bias = bias_all[:, layer_index * HEADS:(layer_index + 1) * HEADS]
            current, operands = layer_global(current, bias, key_valid, offsets_all[layer_index], w_qkvg[layer_index], w_out[layer_index], w_up[layer_index], w_down[layer_index])
            saved.append(operands)
            if layer_index + 1 < LAYERS:
                current = lax.optimization_barrier(current)
        return (current, saved)
    output, pullback, saved = jax.vjp(forward, atoms, projected, zero_sets, has_aux=True)
    grad_atoms, grad_projected, grad_offsets = pullback(cotangent)
    scale = 1.0 / math.sqrt(ATOMS)
    grad_qkvg = jnp.stack([outer_sum(saved[i][0], grad_offsets[i][0]) for i in range(LAYERS)]) * scale
    grad_out = jnp.stack([outer_sum(saved[i][1], grad_offsets[i][1]) for i in range(LAYERS)]) * scale
    grad_up = jnp.stack([outer_sum(saved[i][2], grad_offsets[i][2]) for i in range(LAYERS)]) * scale
    grad_down = jnp.stack([outer_sum(saved[i][3], grad_offsets[i][3]) for i in range(LAYERS)]) * scale
    grad_pair_w = jnp.einsum('gtuc,ghtu->ch', tiles, grad_projected, precision=lax.Precision.HIGHEST) * scale
    grad_tiles = jnp.einsum('ghtu,ch->gtuc', grad_projected, w_pair32, precision=lax.Precision.HIGHEST).astype(jnp.bfloat16)

    def place_tile(tile_args):
        group_index, tile_grad = tile_args
        columns = jnp.arange(NTOK, dtype=jnp.int32) - (group_index * TOK_DEV - TOK_DEV)
        inside = (columns >= 0) & (columns < 3 * TOK_DEV)
        taken = jnp.take(tile_grad, jnp.clip(columns, 0, 3 * TOK_DEV - 1).astype(jnp.int32), axis=1)
        return jnp.where(inside[None, :, None], taken, jnp.zeros_like(taken))
    grad_pair = lax.map(place_tile, (jnp.arange(groups, dtype=jnp.int32), grad_tiles)).reshape(NTOK, NTOK, CPAIR)
    return (output, grad_atoms, grad_pair, grad_qkvg, grad_out, grad_up, grad_down, grad_pair_w)
```

```python
from functools import partial
import math

import jax
import jax.numpy as jnp
from jax import lax
from jax.experimental import pallas as pl
from jax.experimental.pallas import tpu as pltpu
from jax.sharding import PartitionSpec as P

Q_BLOCK = 32
K_BLOCK = 128
HALO = 48
UNIT = 16
MESH = pl.DeviceIdType.MESH


class Reducer:
    def __init__(self, sizes, chips, cols, parts, from_core, half, inbox, totals, sems):
        self.sizes, self.chips, self.cols = sizes, chips, cols
        self.parts, self.from_core, self.half = parts, from_core, half
        self.inbox, self.totals, self.sems = inbox, totals, sems
        seq, col = lax.axis_index("seq"), lax.axis_index("col")
        self.core = lax.rem(seq, 2)
        self.chip = lax.div(seq, 2) * cols + col
        self.sibling = (seq + 1 - 2 * self.core, col)
        self.offsets = [sum(sizes[:i]) % chips for i in range(len(sizes))]

    def device(self, chip):
        return (lax.div(chip, self.cols) * 2 + self.core, lax.rem(chip, self.cols))

    def own(self, p):
        return lax.rem(self.chip - self.offsets[p] + self.chips, self.chips)

    def targets(self):
        everyone = [self.sibling]
        return everyone

    def pair_copy(self, p):
        return pltpu.make_async_remote_copy(
            self.parts[p].at[1 - self.core], self.from_core[p],
            self.sems.at[0, p], self.sems.at[1, p],
            device_id=self.sibling, device_id_type=MESH)

    def back_copy(self, p):
        mine = self.totals[p].at[self.core]
        return pltpu.make_async_remote_copy(
            mine, mine, self.sems.at[6, p], self.sems.at[7, p],
            device_id=self.sibling, device_id_type=MESH)

    def start(self, p):
        self.pair_copy(p).start()

    def scatter(self, p):
        self.pair_copy(p).wait()
        n = self.sizes[p]
        self.half[p][...] = (
            self.parts[p][self.core].astype(jnp.float32) + self.from_core[p][...].astype(jnp.float32)
        ).astype(jnp.bfloat16)
        first = lax.rem(self.chip, n)

        @pl.loop(0, n)
        def _(i):
            unit = lax.rem(first + i, n)
            to = lax.rem(unit + self.offsets[p], self.chips)
            slot = lax.rem(self.chip - to + self.chips, self.chips)

            @pl.when(slot != 0)
            def _():
                pltpu.make_async_remote_copy(
                    self.half[p].at[pl.ds(unit * UNIT, UNIT)], self.inbox[p].at[slot - 1],
                    self.sems.at[2, p], self.sems.at[3, p],
                    device_id=self.device(to), device_id_type=MESH).start()

    def gather(self, p):
        unit = self.own(p)

        @pl.when(unit < self.sizes[p])
        def _():
            box = self.inbox[p]
            pltpu.make_async_copy(box, box, self.sems.at[3, p]).wait()
            rows = pl.ds(unit * UNIT, UNIT)
            total = self.half[p][rows].astype(jnp.float32) + jnp.sum(box[...].astype(jnp.float32), axis=0)
            mine = self.totals[p].at[self.core, rows]
            mine[...] = total.astype(jnp.bfloat16)

            @pl.loop(1, self.chips)
            def _(i):
                pltpu.make_async_remote_copy(
                    mine, mine, self.sems.at[4, p], self.sems.at[5, p],
                    device_id=self.device(lax.rem(self.chip + i, self.chips)), device_id_type=MESH).start()

    def spread(self, p):
        n = self.sizes[p]
        mine = self.totals[p].at[self.core]
        unit = self.own(p)

        def arrived(count):
            if count:
                block = mine.at[pl.ds(0, count * UNIT)]
                pltpu.make_async_copy(block, block, self.sems.at[5, p]).wait()

        @pl.when(unit < n)
        def _():
            arrived(n - 1)

        @pl.when(unit >= n)
        def _():
            arrived(n)

        self.back_copy(p).start()

    def finish(self, p):
        n = self.sizes[p]
        self.back_copy(p).wait()
        unit = self.own(p)

        def sent(count):
            if count:
                block = self.half[p].at[pl.ds(0, count * UNIT)]
                pltpu.make_async_copy(block, block, self.sems.at[2, p]).wait()

        @pl.when(unit < n)
        def _():
            sent(n - 1)
            box = self.inbox[p]
            pltpu.make_async_copy(box, box, self.sems.at[4, p]).wait()

        @pl.when(unit >= n)
        def _():
            sent(n)


def reducer_scratch(sizes, chips):
    rows = [n * UNIT for n in sizes]
    return dict(
        from_core=[pltpu.VMEM((r, 128), jnp.bfloat16) for r in rows],
        half=[pltpu.VMEM((r, 128), jnp.bfloat16) for r in rows],
        inbox=[pltpu.VMEM((chips - 1, UNIT, 128), jnp.bfloat16) for r in rows],
        sems=pltpu.SemaphoreType.DMA((8, len(sizes))),
    )


def greet(devices, count):
    barrier = pltpu.get_barrier_semaphore()
    for device in devices:
        pl.semaphore_signal(barrier, inc=1, device_id=device, device_id_type=MESH)
    pl.semaphore_wait(barrier, count)


def reduce_kernel(sizes, chips, cols, *refs):
    count = len(sizes)
    parts, totals = refs[:count], refs[count : 2 * count]
    from_core, half, inbox = (refs[(2 + i) * count : (3 + i) * count] for i in range(3))
    work = Reducer(sizes, chips, cols, parts, from_core, half, inbox, totals, refs[5 * count])
    barrier = pltpu.get_barrier_semaphore()
    pl.semaphore_signal(barrier, inc=1, device_id=work.sibling, device_id_type=MESH)

    @pl.loop(1, chips)
    def _(i):
        chip = lax.rem(work.chip + i, chips)
        pl.semaphore_signal(barrier, inc=1, device_id=work.device(chip), device_id_type=MESH)

    pl.semaphore_wait(barrier, chips)
    for step in (work.start, work.scatter, work.gather, work.spread, work.finish):
        for p in range(count):
            step(p)


def all_sum(pieces, chips, cols):
    sizes = [piece.shape[1] // UNIT for piece in pieces]
    scratch = reducer_scratch(sizes, chips)
    return pl.pallas_call(
        partial(reduce_kernel, sizes, chips, cols),
        out_shape=[jax.ShapeDtypeStruct(piece.shape, jnp.bfloat16) for piece in pieces],
        in_specs=[pl.BlockSpec(memory_space=pltpu.VMEM)] * len(pieces),
        out_specs=[pl.BlockSpec(memory_space=pltpu.VMEM)] * len(pieces),
        scratch_shapes=[*scratch["from_core"], *scratch["half"], *scratch["inbox"], scratch["sems"]],
        compiler_params=pltpu.CompilerParams(
            collective_id=0, has_side_effects=True, vmem_limit_bytes=32 * 1024 * 1024
        ),
    )(*pieces)


def shortened(shard):
    return jax.tree.map(lambda a: a.astype(jnp.bfloat16) if a.dtype == jnp.float32 else a, shard)


def padded(cells, sides, width):
    for axis, dim in sides:
        count = lax.axis_size(axis)
        ends = count - 1
        head = lax.slice_in_dim(cells, 0, width, axis=dim)
        tail = lax.slice_in_dim(cells, cells.shape[dim] - width, cells.shape[dim], axis=dim)
        cells = jnp.concatenate(
            [
                lax.ppermute(tail, axis, [(i, (i + 1) % count) for i in range(ends)]),
                cells,
                lax.ppermute(head, axis, [((i + 1) % count, i) for i in range(ends)]),
            ],
            axis=dim,
        )
    return cells


def layer_norm(vector):
    average = jnp.mean(vector, axis=-1, keepdims=True)
    centred = vector - average
    spread = jnp.mean(centred * centred, axis=-1, keepdims=True)
    return centred * lax.rsqrt(spread + 1e-05)


def project(resid_in, offset, w_qkvg_l):
    normed = layer_norm(resid_in).astype(jnp.bfloat16)
    pre_act = jnp.dot(normed, w_qkvg_l, preferred_element_type=jnp.float32) + offset
    feature_width = resid_in.shape[1]
    queries = pre_act[:, :feature_width].astype(jnp.bfloat16)
    key_value = pre_act[:, feature_width : 3 * feature_width].astype(jnp.bfloat16)
    queries, key_value = lax.optimization_barrier((queries, key_value))
    gate_act = jax.nn.sigmoid(pre_act[:, 3 * feature_width :])
    return ((queries, key_value, gate_act), normed)


def attend(queries, windows, bias, key_valid):
    blocks = windows.shape[0]
    head_count = bias.shape[1]
    feature_width = queries.shape[1]
    head_dim = feature_width // head_count
    query_part = (
        queries.astype(jnp.bfloat16)
        .astype(jnp.float32)
        .reshape(blocks, Q_BLOCK, head_count, head_dim)
    )
    window_half = windows.astype(jnp.bfloat16).astype(jnp.float32)
    key_part = window_half[:, :, :feature_width].reshape(blocks, K_BLOCK, head_count, head_dim)
    value_part = window_half[:, :, feature_width:].reshape(blocks, K_BLOCK, head_count, head_dim)
    scores = jnp.einsum("bihd,bkhd->bhik", query_part, key_part, preferred_element_type=jnp.float32)
    scores = scores * (1.0 / math.sqrt(head_dim)) + bias
    scores = jnp.where(key_valid[:, None, None, :], scores, -1e30)
    largest = lax.stop_gradient(jnp.max(scores, axis=-1, keepdims=True))
    weights = jnp.exp(scores - largest)
    weights = (weights / jnp.sum(weights, axis=-1, keepdims=True)).astype(jnp.bfloat16)
    mixed = jnp.einsum(
        "bhik,bkhd->bihd",
        weights.astype(jnp.float32),
        value_part,
        preferred_element_type=jnp.float32,
    )
    return mixed.reshape(blocks * Q_BLOCK, feature_width)


def finish(mixed, gate_act, resid_in, offsets, w_out_l, w_up_l, w_down_l):
    hidden_width = w_down_l.shape[0]
    gated = (mixed * gate_act).astype(jnp.bfloat16)
    attn_sum = jnp.dot(gated, w_out_l, preferred_element_type=jnp.float32) + offsets[1]
    residual = resid_in + attn_sum
    normed_two = layer_norm(residual).astype(jnp.bfloat16)
    up_both = jnp.dot(normed_two, w_up_l, preferred_element_type=jnp.float32) + offsets[2]
    hidden = (jax.nn.silu(up_both[:, :hidden_width]) * up_both[:, hidden_width:]).astype(
        jnp.bfloat16
    )
    result = residual + jnp.dot(hidden, w_down_l, preferred_element_type=jnp.float32) + offsets[3]
    return (result.astype(jnp.bfloat16), (gated, normed_two, hidden))


def outer_sum(left, right):
    return jnp.dot(left.astype(jnp.float32).T, right, precision=lax.Precision.HIGHEST)


def per_device(atoms, cotangent, token_counts, pair, w_qkvg, w_out, w_up, w_down, w_pair):
    seq_count = lax.axis_size("seq")
    col_count = lax.axis_size("col")
    groups = seq_count * col_count
    seq_index = lax.axis_index("seq")
    col_index = lax.axis_index("col")
    group_index = seq_index * col_count + col_index
    atom_dev = atoms.shape[0]
    feature_width = atoms.shape[1]
    tok_dev = token_counts.shape[1]
    layers = w_qkvg.shape[0]
    table_count = w_pair.shape[1]
    head_count = table_count // layers
    hidden_width = w_down.shape[1]
    blocks = atom_dev // Q_BLOCK
    position = jnp.arange(atom_dev, dtype=jnp.int32)

    def group_tokens(which):
        safe = jnp.clip(which, 0, groups - 1)
        counts = lax.dynamic_index_in_dim(token_counts, safe, 0, keepdims=False)
        token_ends = jnp.cumsum(counts)
        return jnp.sum((token_ends[None, :] <= position[:, None]).astype(jnp.int32), axis=1)

    own_token = group_tokens(group_index)
    ext_token = jnp.concatenate(
        [
            group_tokens(group_index - 1)[atom_dev - HALO :],
            own_token + tok_dev,
            group_tokens(group_index + 1)[:HALO] + 2 * tok_dev,
        ]
    )
    ext_position = group_index * atom_dev - HALO + jnp.arange(atom_dev + 2 * HALO, dtype=jnp.int32)
    ext_valid = (ext_position >= 0) & (ext_position < atom_dev * groups)
    window_index = (
        jnp.arange(blocks, dtype=jnp.int32)[:, None] * Q_BLOCK
        + jnp.arange(K_BLOCK, dtype=jnp.int32)[None, :]
    )
    key_hot = (ext_token[:, None] == jnp.arange(3 * tok_dev, dtype=jnp.int32)[None, :]).astype(
        jnp.float32
    )[window_index]
    query_hot = (own_token[:, None] == jnp.arange(tok_dev, dtype=jnp.int32)[None, :]).astype(
        jnp.float32
    )
    query_hot = query_hot.reshape(blocks, Q_BLOCK, tok_dev)
    key_valid = ext_valid[window_index]

    def block_bias(table):
        rows_part = jnp.einsum("bit,htu->bhiu", query_hot, table, precision=lax.Precision.HIGHEST)
        return jnp.einsum("bhiu,bku->bhik", rows_part, key_hot, precision=lax.Precision.HIGHEST)

    row_count = pair.shape[0]
    col_width = pair.shape[1]
    window = tok_dev * (col_count + 4)
    window_start = seq_index * row_count - 2 * tok_dev - col_index * col_width
    local_cols = window_start + jnp.arange(window, dtype=jnp.int32)
    inside = (local_cols >= 0) & (local_cols < col_width)
    pair_piece = jnp.take(pair, jnp.clip(local_cols, 0, col_width - 1), axis=1)
    pair_piece = jnp.where(inside[None, :, None], pair_piece, jnp.zeros_like(pair_piece))
    reader_offset = (col_index + 1) * tok_dev
    w_pair32 = w_pair.astype(jnp.float32)
    piece_heads = jnp.einsum(
        "rwc,ch->hrw", pair_piece.astype(jnp.float32), w_pair32, preferred_element_type=jnp.float32
    )
    shares = lax.psum_scatter(piece_heads, "col", scatter_dimension=1, tiled=True)
    projected = lax.dynamic_slice_in_dim(shares, reader_offset, 3 * tok_dev, 2)

    def attention_layer(
        queries,
        key_ext,
        gate_act,
        table,
        resid_in,
        off_out,
        off_up,
        off_down,
        w_out_l,
        w_up_l,
        w_down_l,
    ):
        windows = key_ext[window_index]
        mixed = attend(queries.astype(jnp.float32), windows, block_bias(table), key_valid)
        return finish(
            mixed, gate_act, resid_in, (None, off_out, off_up, off_down), w_out_l, w_up_l, w_down_l
        )

    zero_qkvg = jnp.zeros((atom_dev, 4 * feature_width), jnp.float32)
    zero_out = jnp.zeros((atom_dev, feature_width), jnp.float32)
    zero_up = jnp.zeros((atom_dev, 2 * hidden_width), jnp.float32)
    zero_down = jnp.zeros((atom_dev, feature_width), jnp.float32)
    current = atoms
    pullbacks = []
    for layer_index in range(layers):
        resid_in = current.astype(jnp.float32)
        (queries, key_value, gate_act), proj_back, normed = jax.vjp(
            partial(project, w_qkvg_l=w_qkvg[layer_index]), resid_in, zero_qkvg, has_aux=True
        )
        key_ext = padded(shortened(key_value), ((("seq", "col"), 0),), HALO).astype(key_value.dtype)
        table = projected[layer_index * head_count : (layer_index + 1) * head_count]
        result, attn_back, operands = jax.vjp(
            partial(
                attention_layer,
                w_out_l=w_out[layer_index],
                w_up_l=w_up[layer_index],
                w_down_l=w_down[layer_index],
            ),
            queries,
            key_ext.astype(jnp.float32),
            gate_act,
            table,
            resid_in,
            zero_out,
            zero_up,
            zero_down,
            has_aux=True,
        )
        pullbacks.append((proj_back, attn_back, normed, operands))
        current = result
        if layer_index + 1 < layers:
            current = lax.optimization_barrier(current)
    grad_current = cotangent
    grad_tables = [None] * layers
    collected = [None] * layers
    for layer_index in reversed(range(layers)):
        proj_back, attn_back, normed, operands = pullbacks[layer_index]
        gated, normed_two, hidden = operands
        d_queries, d_key_ext, d_gate, d_table, d_resid_a, d_off_out, d_off_up, d_off_down = (
            attn_back(grad_current)
        )
        edges = jnp.concatenate([d_key_ext[:HALO], d_key_ext[HALO + atom_dev :]], axis=0)
        moved = padded(edges, ((("seq", "col"), 0),), HALO)
        from_prev = moved[:HALO]
        from_next = moved[moved.shape[0] - HALO :]
        d_key_value = (
            d_key_ext[HALO : HALO + atom_dev]
            + jnp.pad(from_prev, ((0, atom_dev - HALO), (0, 0)))
            + jnp.pad(from_next, ((atom_dev - HALO, 0), (0, 0)))
        )
        d_resid_p, d_off_qkvg = proj_back((d_queries, d_key_value.astype(jnp.bfloat16), d_gate))
        grad_current = (d_resid_a + d_resid_p).astype(jnp.bfloat16)
        layer_grads = (
            outer_sum(normed, d_off_qkvg),
            outer_sum(gated, d_off_out),
            outer_sum(normed_two, d_off_up),
            outer_sum(hidden, d_off_down),
        )
        collected[layer_index] = layer_grads
        grad_tables[layer_index] = d_table
    d_projected = jnp.concatenate(grad_tables, axis=0)
    placed = jnp.zeros((table_count, tok_dev, window), jnp.float32)
    placed = lax.dynamic_update_slice_in_dim(placed, d_projected, reader_offset, 2)
    gathered = lax.all_gather(placed, "col", axis=1, tiled=True)
    grad_window = jnp.einsum(
        "hrw,ch->rwc", gathered, w_pair32, precision=lax.Precision.HIGHEST
    ).astype(jnp.bfloat16)
    grad_pair_w = jnp.einsum(
        "rwc,hrw->ch", pair_piece.astype(jnp.float32), gathered, precision=lax.Precision.HIGHEST
    )
    shard_cols = jnp.arange(col_width, dtype=jnp.int32) - window_start
    inside_shard = (shard_cols >= 0) & (shard_cols < window)
    grad_pair = jnp.take(grad_window, jnp.clip(shard_cols, 0, window - 1), axis=1)
    grad_pair = jnp.where(inside_shard[None, :, None], grad_pair, jnp.zeros_like(grad_pair))
    pieces = []
    for i in range(layers):
        qkvg, out, up, down = collected[i]
        blocks_of = [qkvg[:, j : j + 128] for j in range(0, qkvg.shape[1], 128)] + [out]
        blocks_of += [up[:, j : j + 128] for j in range(0, up.shape[1], 128)] + [down]
        pieces.append(jnp.concatenate(blocks_of, axis=0).astype(jnp.bfloat16).reshape(2, -1, 128))
    spare = 2 * UNIT - table_count
    pieces.append(
        jnp.pad(grad_pair_w.T, ((0, spare), (0, 0))).astype(jnp.bfloat16).reshape(2, UNIT, 128)
    )
    sums = [p.astype(jnp.float32).reshape(-1, 128) for p in all_sum(pieces, groups // 2, col_count)]
    fw = feature_width
    totals = (
        jnp.stack([jnp.concatenate([p[j * fw : (j + 1) * fw] for j in range(4)], 1) for p in sums[:layers]]),
        jnp.stack([p[4 * fw : 5 * fw] for p in sums[:layers]]),
        jnp.stack([jnp.concatenate([p[j * fw : (j + 1) * fw] for j in range(5, 9)], 1) for p in sums[:layers]]),
        jnp.stack([p[9 * fw : 11 * fw] for p in sums[:layers]]),
        sums[layers][:table_count].T,
    )
    scale = 1.0 / math.sqrt(atom_dev * groups)
    return (
        current,
        grad_current,
        grad_pair,
        totals[0] * scale,
        totals[1] * scale,
        totals[2] * scale,
        totals[3] * scale,
        totals[4] * scale,
    )


def solution(mesh):
    return jax.shard_map(
        per_device,
        mesh=mesh,
        in_specs=(
            P(("seq", "col"), None),
            P(("seq", "col"), None),
            P(),
            P("seq", "col", None),
            P(),
            P(),
            P(),
            P(),
            P(),
        ),
        out_specs=(
            P(("seq", "col"), None),
            P(("seq", "col"), None),
            P("seq", "col", None),
            P(),
            P(),
            P(),
            P(),
            P(),
        ),
        check_vma=False,
    )
```
